32 devices in a mesh: row: 4 (over x, core), col: 8 (over z, y).
Axes of the slice: x: 2, y: 2, z: 4, core: 2. Of those that a mesh axis runs over, the one named last changes fastest.
Arguments:
- trajectory_activations: bfloat16 [640, 5120], P('row', 'col'), may hold values from -6 to 6
- kept_clusters_mask: int32 [16], replicated, may hold values from 0 to 1, as said below
- piece_receiving_entry: int32 [80], replicated, may hold values from 0 to 3, as said below
- piece_opening_position: int32 [80], replicated, may hold values from 0 to 72, as said below
- switching_coefficients: bfloat16 [27648, 5120], P('row', 'col'), may hold values from -0.078125 to 0.078125
- expansion_coefficients: bfloat16 [27648, 5120], P('row', 'col'), may hold values from -0.078125 to 0.078125
- contraction_coefficients: bfloat16 [27648, 5120], P('row', 'col'), may hold values from -0.0390625 to 0.0390625
- adjoint_vector: bfloat16 [320, 5120], P('row', 'col'), may hold values from -1.5 to 1.5
Outputs:
- mixed: bfloat16 [320, 5120], P('row', 'col')
- grad_input: bfloat16 [320, 5120], P('row', 'col')
- grad_w_gate: float32 [27648, 5120], P('row', 'col')
- grad_w_up: float32 [27648, 5120], P('row', 'col')
- grad_w_down: float32 [27648, 5120], P('row', 'col')
The draws below stay inside these ranges and needn't reach their ends.
Inputs may be any that keep to these rules, and one draw needn't show every extreme that they name: `kept_clusters_mask`: exactly 8 groups are kept, among them all 4 groups of one row index of the rollout. `piece_receiving_entry`: only entries of kept groups' blocks matter. Each row index of the packed batch receives the blocks of exactly 2 kept groups. The kept blocks of one row index of the rollout send at most 5 blocks to one row index of the packed batch, and in every draw some send exactly 5. `piece_opening_position`: only entries of kept groups' blocks matter. Each is a multiple of 8; the kept blocks cover every row index's 80 packed tokens exactly once.
All inputs are finite; a program needn't handle non-finite values.
Results may differ from the reference program's by a relative error of at most 0.004.
Values may be sent and summed in bfloat16 or wider, within the bound.
A program may use at most 192 MiB of HBM per device.

```python
import jax
import jax.numpy as jnp

D = 5120
FF = 27648
TOK_ROW = 80
BLOCK = 8
GRP_ROW = 4
CLUSTER_PIECES = 5
TOKENS = 320
ROLL = 640
GROUPS = 16
KEEP = 8
BLOCKS = 80


def packing_plan(key):
    base = jax.random.fold_in(key, 4242)
    keys = jax.random.split(base, 6)
    n_rows = TOKENS // TOK_ROW
    slots = TOK_ROW // BLOCK
    owner = jnp.arange(GROUPS, dtype=jnp.int32) // GRP_ROW
    busiest = jax.random.randint(keys[0], (), 0, n_rows, dtype=jnp.int32)
    priority = jax.random.permutation(keys[1], GROUPS).astype(jnp.int32)
    priority = jnp.where(owner == busiest, priority - GROUPS, priority)
    ranking = jnp.sum((priority[None, :] < priority[:, None]).astype(jnp.int32), axis=1)
    kept = (ranking < KEEP).astype(jnp.int32)
    position = jnp.cumsum(kept) - 1
    dest_perm = jax.random.permutation(keys[2], n_rows).astype(jnp.int32)
    group_dest = dest_perm[jnp.remainder(position, n_rows)]
    group_half = position // n_rows
    slot_table = jax.random.permutation(keys[3], jnp.tile(jnp.arange(slots, dtype=jnp.int32)[None, :], (n_rows, 1)), axis=1, independent=True)
    block_group = jnp.arange(BLOCKS, dtype=jnp.int32) // CLUSTER_PIECES
    block_part = jnp.arange(BLOCKS, dtype=jnp.int32) % CLUSTER_PIECES
    survival_indicator = kept[block_group]
    dest_live = group_dest[block_group]
    slot_index = jnp.clip(group_half[block_group] * CLUSTER_PIECES + block_part, 0, slots - 1)
    offset_live = BLOCK * slot_table[dest_live, slot_index]
    dest_other = jax.random.randint(keys[4], (BLOCKS,), 0, n_rows, dtype=jnp.int32)
    offset_other = BLOCK * jax.random.randint(keys[5], (BLOCKS,), 0, slots, dtype=jnp.int32)
    dest_final = jnp.where(survival_indicator == 1, dest_live, dest_other).astype(jnp.int32)
    offset_final = jnp.where(survival_indicator == 1, offset_live, offset_other).astype(jnp.int32)
    return (kept, dest_final, offset_final)


def draw_kept_clusters_mask(key, part):
    return packing_plan(key)[0]


def draw_piece_receiving_entry(key, part):
    return packing_plan(key)[1]


def draw_piece_opening_position(key, part):
    return packing_plan(key)[2]


def level_of(stream_key, shape, pieces, smallest, high):
    gain, own = 1.0, jax.random.fold_in(stream_key, 6)
    for axis_at, blocks in pieces:
        draws = jnp.exp(jax.random.uniform(jax.random.fold_in(own, axis_at), (blocks,), jnp.float32, smallest / len(pieces), high / len(pieces)))
        gain = gain * jnp.repeat(draws, shape[axis_at] // blocks).reshape([-1 if axis == axis_at else 1 for axis in range(len(shape))])
    return gain


def scatter_about(own_key, dims, scale, limit, cuts=(), kind=jnp.bfloat16):
    values = jax.random.normal(own_key, dims, jnp.float32) * scale
    if len(cuts) > 0:
        values = level_of(own_key, dims, cuts, -0.22, 0.18) * values
    return jnp.clip(values, min=-limit, max=limit).astype(kind)


def setup_inputs(seed: int = 0) -> dict:
    seeds = jax.random.split(jax.random.key(seed), 9)
    trajectory_activations = scatter_about(seeds[0], (ROLL, D), 1.0, 6.0, ((0, 4), (1, 8)))
    kept_clusters_mask = draw_kept_clusters_mask(jax.random.fold_in(seeds[8], 71), 0)
    piece_receiving_entry = draw_piece_receiving_entry(jax.random.fold_in(seeds[8], 71), 0)
    piece_opening_position = draw_piece_opening_position(jax.random.fold_in(seeds[8], 71), 0)
    switching_coefficients = scatter_about(seeds[4], (FF, D), D ** -0.5, 0.078125, ((0, 4), (1, 8)))
    expansion_coefficients = scatter_about(seeds[5], (FF, D), D ** -0.5, 0.078125, ((0, 4), (1, 8)))
    contraction_coefficients = scatter_about(seeds[6], (FF, D), FF ** -0.5, 0.0390625, ((0, 4), (1, 8)))
    adjoint_vector = scatter_about(seeds[7], (TOKENS, D), 0.25, 1.5, ((0, 4), (1, 8)))
    return {"trajectory_activations": trajectory_activations, "kept_clusters_mask": kept_clusters_mask, "piece_receiving_entry": piece_receiving_entry, "piece_opening_position": piece_opening_position, "switching_coefficients": switching_coefficients, "expansion_coefficients": expansion_coefficients, "contraction_coefficients": contraction_coefficients, "adjoint_vector": adjoint_vector}


def dense_emitters(kept_clusters_mask, piece_receiving_entry, piece_opening_position):
    blocks = piece_receiving_entry.shape[0]
    cluster_mapping = jnp.arange(blocks, dtype=jnp.int32) // CLUSTER_PIECES
    survival_indicator = kept_clusters_mask[cluster_mapping] == 1
    first_token = (piece_receiving_entry * TOK_ROW + piece_opening_position).astype(jnp.int32)
    within = jnp.arange(BLOCK, dtype=jnp.int32)
    target = jnp.where(survival_indicator[:, None], first_token[:, None] + within[None, :], TOKENS)
    target = target.reshape(-1).astype(jnp.int32)
    source = jnp.arange(blocks * BLOCK, dtype=jnp.int32)
    return jnp.zeros((TOKENS,), jnp.int32).at[target].set(source, mode="drop")


def reference(trajectory_activations, kept_clusters_mask, piece_receiving_entry, piece_opening_position, switching_coefficients, expansion_coefficients, contraction_coefficients, adjoint_vector):
    emitter_sequence = dense_emitters(kept_clusters_mask, piece_receiving_entry, piece_opening_position)
    packed = jnp.take(trajectory_activations, emitter_sequence, axis=0)
    gate_proj = jnp.dot(packed, switching_coefficients.T, preferred_element_type=jnp.float32)
    up_proj = jnp.dot(packed, expansion_coefficients.T, preferred_element_type=jnp.float32)
    sig_gate = jax.nn.sigmoid(gate_proj)
    hidden = (gate_proj * sig_gate * up_proj).astype(jnp.bfloat16)
    mixed = (packed.astype(jnp.float32) + jnp.dot(hidden, contraction_coefficients, preferred_element_type=jnp.float32)).astype(jnp.bfloat16)
    grad_hidden = jnp.dot(adjoint_vector, contraction_coefficients.T, preferred_element_type=jnp.float32)
    grad_gate = (grad_hidden * up_proj * sig_gate * (1.0 + gate_proj * (1.0 - sig_gate))).astype(jnp.bfloat16)
    grad_up = (grad_hidden * gate_proj * sig_gate).astype(jnp.bfloat16)
    grad_w_down = jnp.dot(hidden.T, adjoint_vector, preferred_element_type=jnp.float32)
    grad_w_gate = jnp.dot(grad_gate.T, packed, preferred_element_type=jnp.float32)
    grad_w_up = jnp.dot(grad_up.T, packed, preferred_element_type=jnp.float32)
    back_sum = jnp.dot(grad_gate, switching_coefficients, preferred_element_type=jnp.float32) + jnp.dot(grad_up, expansion_coefficients, preferred_element_type=jnp.float32)
    grad_input = (adjoint_vector.astype(jnp.float32) + back_sum).astype(jnp.bfloat16)
    return mixed, grad_input, grad_w_gate, grad_w_up, grad_w_down
```

```python
import math

import jax
import jax.numpy as jnp
from jax import lax
from jax.sharding import PartitionSpec as P

TOK_ROW = 80
BLOCK = 8
CLUSTER_PIECES = 5
X_MAX, W_MAX, DOWN_MAX, COT_MAX = 6.0, 0.078125, 0.0390625, 1.5


def ring_places(count):
    if count % 4 or count < 8:
        return list(range(count))
    lines, width = 4, count // 4
    ring = [0]
    for line in range(lines):
        across = list(range(1, width))
        ring += [line * width + c for c in (across if line % 2 == 0 else across[::-1])]
    ring += [line * width for line in range(lines - 1, 0, -1)]
    places = [0] * count
    for place, index in enumerate(ring):
        places[index] = place
    return places


def half_scale(bound):
    return 2.0 ** math.floor(math.log2(65504.0 / (1.05 * bound)))


def dot_rows(tokens, units):
    return lax.dot_general(
        tokens, units, (((1,), (1,)), ((), ())), preferred_element_type=jnp.float32
    )


def dot_units(tokens, units):
    return lax.dot_general(
        tokens, units, (((1,), (0,)), ((), ())), preferred_element_type=jnp.float32
    )


def dot_tokens(first_op, second_op):
    return lax.dot_general(
        first_op, second_op, (((0,), (0,)), ((), ())), preferred_element_type=jnp.float32
    )


def per_device(
    trajectory_activations,
    kept_clusters_mask,
    piece_receiving_entry,
    piece_opening_position,
    switching_coefficients,
    expansion_coefficients,
    contraction_coefficients,
    adjoint_vector,
):
    row_count = lax.axis_size("row")
    col_count = lax.axis_size("col")
    row_here = lax.axis_index("row")
    feature_cols = trajectory_activations.shape[1]
    roll_rows = trajectory_activations.shape[0]
    tokens = row_count * TOK_ROW
    units = switching_coefficients.shape[0] // col_count
    width = feature_cols * col_count

    both = lax.all_gather(
        jnp.concatenate((trajectory_activations, adjoint_vector), axis=0), "row", axis=0
    )
    roll = both[:, :roll_rows].reshape(row_count * roll_rows, feature_cols)
    cot_panel = both[:, roll_rows:].reshape(tokens, feature_cols)

    live = jnp.broadcast_to(
        kept_clusters_mask[:, None] == 1, (kept_clusters_mask.shape[0], CLUSTER_PIECES)
    ).reshape(-1)
    first = jnp.where(live, piece_receiving_entry * TOK_ROW + piece_opening_position, -BLOCK)
    target = (first[:, None] + jnp.arange(BLOCK, dtype=jnp.int32)[None, :]).reshape(-1)
    selector = (jnp.arange(tokens, dtype=jnp.int32)[:, None] == target[None, :]).astype(
        jnp.bfloat16
    )
    x_panel = jnp.dot(selector, roll, preferred_element_type=jnp.float32).astype(jnp.bfloat16)

    places = ring_places(col_count)
    ring = [0] * col_count
    for index, place in enumerate(places):
        ring[place] = index
    col_here = lax.axis_index("col")
    here = jnp.int32(0)
    for index, place in enumerate(places):
        here = here + jnp.where(col_here == index, place, 0)
    steps = {
        way: [(ring[p], ring[(p + way) % col_count]) for p in range(col_count)] for way in (1, -1)
    }
    longer = col_count // 2
    shorter = col_count - 1 - longer

    def at(offset):
        return lax.rem(here + (offset + col_count) % col_count, col_count)

    def share(weight, owner):
        return lax.dynamic_slice_in_dim(weight, owner * units, units, 0)

    def reduce_to_owner(panel, weight, scale, hops_up):
        total = dot_rows(panel, share(weight, here))
        for way, hops in ((1, hops_up), (-1, col_count - 1 - hops_up)):
            carried = None
            for step in range(hops):
                term = dot_rows(panel, share(weight, at(way * (hops - step)))) * scale
                if carried is not None:
                    term = term + carried.astype(jnp.float32)
                carried = lax.ppermute(term.astype(jnp.float16), "col", steps[way])
            total = total + carried.astype(jnp.float32) * (1.0 / scale)
        return total

    def spread(mine, hops_up):
        held = [(here, mine)]
        for way, hops in ((1, hops_up), (-1, col_count - 1 - hops_up)):
            moving = mine
            for step in range(hops):
                moving = lax.ppermute(moving, "col", steps[way])
                held.append((at(-way * (step + 1)), moving))
        return held

    grad_hidden = reduce_to_owner(
        cot_panel, contraction_coefficients, half_scale(width * COT_MAX * DOWN_MAX), longer
    )
    proj_scale = half_scale(width * X_MAX * W_MAX)
    gate_proj = reduce_to_owner(x_panel, switching_coefficients, proj_scale, longer)
    up_proj = reduce_to_owner(x_panel, expansion_coefficients, proj_scale, shorter)
    sig_gate = jax.nn.sigmoid(gate_proj)
    hidden = (gate_proj * sig_gate * up_proj).astype(jnp.bfloat16)
    grad_gate = (grad_hidden * up_proj * sig_gate * (1.0 + gate_proj * (1.0 - sig_gate))).astype(
        jnp.bfloat16
    )
    grad_up = (grad_hidden * gate_proj * sig_gate).astype(jnp.bfloat16)

    def outer(held, panel):
        out = jnp.zeros((col_count * units, feature_cols), jnp.float32)
        for owner, part in held:
            out = lax.dynamic_update_slice_in_dim(out, dot_tokens(part, panel), owner * units, 0)
        return out

    def inner(held, weight, total=None):
        for owner, part in held:
            term = dot_units(part, share(weight, owner))
            total = term if total is None else total + term
        return total

    hidden_held = spread(hidden, longer)
    gate_held = spread(grad_gate, shorter)
    up_held = spread(grad_up, longer)
    mixed_part = lax.psum_scatter(
        inner(hidden_held, contraction_coefficients), "row", scatter_dimension=0, tiled=True
    )
    input_sum = inner(up_held, expansion_coefficients, inner(gate_held, switching_coefficients))
    input_part = lax.psum_scatter(input_sum, "row", scatter_dimension=0, tiled=True)
    grad_w_down = outer(hidden_held, cot_panel)
    grad_w_gate = outer(gate_held, x_panel)
    grad_w_up = outer(up_held, x_panel)
    local_rows = lax.dynamic_slice_in_dim(x_panel, row_here * TOK_ROW, TOK_ROW, 0)
    mixed = (local_rows.astype(jnp.float32) + mixed_part).astype(jnp.bfloat16)
    grad_input = (adjoint_vector.astype(jnp.float32) + input_part).astype(jnp.bfloat16)
    return (mixed, grad_input, grad_w_gate, grad_w_up, grad_w_down)


def solution(mesh):
    return jax.shard_map(
        per_device,
        mesh=mesh,
        in_specs=(
            P("row", "col"),
            P(),
            P(),
            P(),
            P("row", "col"),
            P("row", "col"),
            P("row", "col"),
            P("row", "col"),
        ),
        out_specs=(
            P("row", "col"),
            P("row", "col"),
            P("row", "col"),
            P("row", "col"),
            P("row", "col"),
        ),
        check_vma=False,
    )
```

```python
import math

import jax
import jax.numpy as jnp
from jax import lax
from jax.experimental import pallas as pl
from jax.sharding import PartitionSpec as P

TOK_ROW = 80
BLOCK = 8
CLUSTER_PIECES = 5
X_MAX, W_MAX, DOWN_MAX, COT_MAX = 6.0, 0.078125, 0.0390625, 1.5


def ring_places(count):
    if count % 4 or count < 8:
        return list(range(count))
    lines, width = 4, count // 4
    ring = [0]
    for line in range(lines):
        across = list(range(1, width))
        ring += [line * width + c for c in (across if line % 2 == 0 else across[::-1])]
    ring += [line * width for line in range(lines - 1, 0, -1)]
    places = [0] * count
    for place, index in enumerate(ring):
        places[index] = place
    return places


def half_scale(bound):
    return 2.0 ** math.floor(math.log2(65504.0 / (1.05 * bound)))


def dot_rows(tokens, units):
    return lax.dot_general(
        tokens, units, (((1,), (1,)), ((), ())), preferred_element_type=jnp.float32
    )


def dot_units(tokens, units):
    return lax.dot_general(
        tokens, units, (((1,), (0,)), ((), ())), preferred_element_type=jnp.float32
    )


def dot_tokens(first_op, second_op):
    return lax.dot_general(
        first_op, second_op, (((0,), (0,)), ((), ())), preferred_element_type=jnp.float32
    )


def blank(rows, columns):
    def kernel(out_ref):
        pass

    return pl.pallas_call(
        kernel,
        out_shape=jax.ShapeDtypeStruct((rows, columns), jnp.float32),
        out_specs=pl.BlockSpec(memory_space=pl.ANY),
    )()


def per_device(
    trajectory_activations,
    kept_clusters_mask,
    piece_receiving_entry,
    piece_opening_position,
    switching_coefficients,
    expansion_coefficients,
    contraction_coefficients,
    adjoint_vector,
):
    row_count = lax.axis_size("row")
    col_count = lax.axis_size("col")
    row_here = lax.axis_index("row")
    feature_cols = trajectory_activations.shape[1]
    roll_rows = trajectory_activations.shape[0]
    tokens = row_count * TOK_ROW
    units = switching_coefficients.shape[0] // col_count
    width = feature_cols * col_count

    def row_pieces(mine):
        pieces = [mine]
        for ahead in range(1, row_count):
            turn = [((r + ahead) % row_count, r) for r in range(row_count)]
            pieces.append(lax.ppermute(mine, "row", turn))
        return jnp.concatenate(pieces, axis=0)

    def row_sum(partial):
        total = partial[:TOK_ROW]
        for ahead in range(1, row_count):
            turn = [(r, (r + ahead) % row_count) for r in range(row_count)]
            piece = partial[ahead * TOK_ROW : (ahead + 1) * TOK_ROW]
            total = total + lax.ppermute(piece, "row", turn)
        return total

    owners = lax.rem(row_here + jnp.arange(row_count, dtype=jnp.int32), row_count)
    cot_panel = row_pieces(adjoint_vector)

    places = ring_places(col_count)
    ring = [0] * col_count
    for index, place in enumerate(places):
        ring[place] = index
    col_here = lax.axis_index("col")
    here = jnp.int32(0)
    for index, place in enumerate(places):
        here = here + jnp.where(col_here == index, place, 0)
    steps = {
        way: [(ring[p], ring[(p + way) % col_count]) for p in range(col_count)] for way in (1, -1)
    }
    longer = col_count // 2
    shorter = col_count - 1 - longer

    def at(offset):
        return lax.rem(here + (offset + col_count) % col_count, col_count)

    def share(weight, owner):
        return lax.dynamic_slice_in_dim(weight, owner * units, units, 0)

    def first_terms(panel, weight, scale, hops_up):
        return [
            (dot_rows(panel, share(weight, at(way * hops))) * scale).astype(jnp.float16)
            for way, hops in ((1, hops_up), (-1, col_count - 1 - hops_up))
        ]

    def reduce_to_owner(panel, weight, scale, hops_up, begun):
        total = dot_rows(panel, share(weight, here))
        for way, hops, opening in (
            (1, hops_up, begun[0]),
            (-1, col_count - 1 - hops_up, begun[1]),
        ):
            carried = lax.ppermute(opening, "col", steps[way])
            for step in range(1, hops):
                term = dot_rows(panel, share(weight, at(way * (hops - step)))) * scale
                term = term + carried.astype(jnp.float32)
                carried = lax.ppermute(term.astype(jnp.float16), "col", steps[way])
            total = total + carried.astype(jnp.float32) * (1.0 / scale)
        return total

    def spread(mine, hops_up):
        held = [(here, mine)]
        for way, hops in ((1, hops_up), (-1, col_count - 1 - hops_up)):
            moving = mine
            for step in range(hops):
                moving = lax.ppermute(moving, "col", steps[way])
                held.append((at(-way * (step + 1)), moving))
        return held

    back_scale = half_scale(width * COT_MAX * DOWN_MAX)
    begun = first_terms(cot_panel, contraction_coefficients, back_scale, longer)
    rollout, *begun = lax.optimization_barrier((trajectory_activations, *begun))
    grad_hidden = reduce_to_owner(cot_panel, contraction_coefficients, back_scale, longer, begun)

    roll = row_pieces(rollout)
    live = jnp.broadcast_to(
        kept_clusters_mask[:, None] == 1, (kept_clusters_mask.shape[0], CLUSTER_PIECES)
    ).reshape(-1)
    place = lax.rem(piece_receiving_entry - row_here + row_count, row_count)
    first = jnp.where(live, place * TOK_ROW + piece_opening_position, -BLOCK)
    target = (first[:, None] + jnp.arange(BLOCK, dtype=jnp.int32)[None, :]).reshape(
        row_count, roll_rows
    )
    target = jnp.take(target, owners, axis=0).reshape(-1)
    selector = (jnp.arange(tokens, dtype=jnp.int32)[:, None] == target[None, :]).astype(
        jnp.bfloat16
    )
    x_panel = jnp.dot(selector, roll, preferred_element_type=jnp.float32).astype(jnp.bfloat16)

    proj_scale = half_scale(width * X_MAX * W_MAX)
    gate_proj = reduce_to_owner(
        x_panel,
        switching_coefficients,
        proj_scale,
        longer,
        first_terms(x_panel, switching_coefficients, proj_scale, longer),
    )
    up_proj = reduce_to_owner(
        x_panel,
        expansion_coefficients,
        proj_scale,
        shorter,
        first_terms(x_panel, expansion_coefficients, proj_scale, shorter),
    )
    sig_gate = jax.nn.sigmoid(gate_proj)
    hidden = (gate_proj * sig_gate * up_proj).astype(jnp.bfloat16)
    grad_gate = (grad_hidden * up_proj * sig_gate * (1.0 + gate_proj * (1.0 - sig_gate))).astype(
        jnp.bfloat16
    )
    grad_up = (grad_hidden * gate_proj * sig_gate).astype(jnp.bfloat16)

    def outer(held, panel):
        out = blank(col_count * units, feature_cols)
        for owner, part in held:
            out = lax.dynamic_update_slice_in_dim(out, dot_tokens(part, panel), owner * units, 0)
        return out

    def inner(held, weight, total=None):
        for owner, part in held:
            term = dot_units(part, share(weight, owner))
            total = term if total is None else total + term
        return total

    hidden_held = spread(hidden, longer)
    landed = hidden_held[2][1]
    grad_gate, grad_up, landed = lax.optimization_barrier((grad_gate, grad_up, landed))
    hidden_held[2] = (hidden_held[2][0], landed)
    gate_held = spread(grad_gate, shorter)
    up_held = spread(grad_up, longer)
    mixed_part = row_sum(inner(hidden_held, contraction_coefficients))
    input_sum = inner(up_held, expansion_coefficients, inner(gate_held, switching_coefficients))
    input_part = row_sum(input_sum)
    grad_w_down = outer(hidden_held, cot_panel)
    grad_w_gate = outer(gate_held, x_panel)
    grad_w_up = outer(up_held, x_panel)
    mixed = (x_panel[:TOK_ROW].astype(jnp.float32) + mixed_part).astype(jnp.bfloat16)
    grad_input = (adjoint_vector.astype(jnp.float32) + input_part).astype(jnp.bfloat16)
    return (mixed, grad_input, grad_w_gate, grad_w_up, grad_w_down)


def solution(mesh):
    return jax.shard_map(
        per_device,
        mesh=mesh,
        in_specs=(
            P("row", "col"),
            P(),
            P(),
            P(),
            P("row", "col"),
            P("row", "col"),
            P("row", "col"),
            P("row", "col"),
        ),
        out_specs=(
            P("row", "col"),
            P("row", "col"),
            P("row", "col"),
            P("row", "col"),
            P("row", "col"),
        ),
        check_vma=False,
    )
```
